128 devices in a mesh: band: 8 (over x_hi, y), dom: 16 (over x_lo, z, core).
Axes of the slice: x: 4 (x_hi: 2, x_lo: 2; x = x_hi * 2 + x_lo), y: 4, z: 4, core: 2. Of those that a mesh axis runs over, the one named last changes fastest.
Arguments:
- orbitals: bfloat16 [192, 128, 3200], P('band', None, 'dom'), may hold values from -6 to 6
- rotation: bfloat16 [192, 192], P('band'), may hold values from -0.4375 to 0.4375
- potential: float32 [128, 3200], P('dom'), may hold values from -1.5 to 0.5
Outputs:
- filtered: float32 [192, 128, 3200], P('band', 'dom')
The draws below stay inside these ranges and needn't reach their ends.
All inputs are finite; a program needn't handle non-finite values.
Results may differ from the reference program's by a relative error of at most 0.0029.
Values may be sent and summed in bfloat16 or wider, within the bound.
A program may use at most 256 MiB of HBM per device.

```python
import jax
import jax.numpy as jnp
from jax import lax

NB = 192
NY = 80
PASSES = 4
NZ = 128
NXY = 3200


def steps_of(rng, shape, shards, low, top_value):
    gain, own = 1.0, jax.random.fold_in(rng, 6)
    for position, shards_of in shards:
        draws = jnp.exp(jax.random.uniform(jax.random.fold_in(own, position), (shards_of,), jnp.float32, low / len(shards), top_value / len(shards)))
        gain = gain * jnp.repeat(draws, shape[position] // shards_of).reshape([-1 if axis == position else 1 for axis in range(len(shape))])
    return gain


def gaussian(own_key, shape, spread, bound, split=(), kind=jnp.bfloat16):
    loudness = steps_of(own_key, shape, split, -0.22, 0.18) if split else 1.0
    entries = jax.random.normal(own_key, shape, jnp.float32) * spread * loudness
    return jnp.minimum(jnp.maximum(entries, -bound), bound).astype(kind)


def setup_inputs(seed: int = 0) -> dict:
    seeds = jax.random.split(jax.random.key(seed), 4)
    return {
        "orbitals": gaussian(seeds[0], (NB, NZ, NXY), 1.0, 6.0, ((0, 8), (2, 16))),
        "rotation": gaussian(seeds[1], (NB, NB), NB ** -0.5, 0.4375, ((0, 8),)),
        "potential": jnp.clip(-1.5 + 2.0 * jax.random.uniform(seeds[2], (NZ, NXY), jnp.float32) ** steps_of(seeds[2], (NZ, NXY), ((0, 16),), -0.2, 0.2), -1.5, 0.5),
    }


potential_offset = 0.5
near_weight = 2.0 / 3.0
far_weight = 1.0 / 24.0
half_range = 4.25
block_width = 16


def shift_columns(values, offset):
    column_y = jnp.arange(values.shape[-1]) % NY
    source = column_y - offset
    inside = (source >= 0) & (source < NY)
    wrapped = offset - NY if offset > 0 else offset + NY
    return jnp.where(inside, jnp.roll(values, offset, -1), jnp.roll(values, wrapped, -1))


def shifted_operator(extended, potential_rows):
    center = extended[:, 2:-2]
    nearest = extended[:, 1:-3] + extended[:, 3:-1]
    nearest = nearest + jnp.roll(center, NY, -1) + jnp.roll(center, -NY, -1)
    nearest = nearest + shift_columns(center, 1) + shift_columns(center, -1)
    second = extended[:, :-4] + extended[:, 4:]
    second = second + jnp.roll(center, 2 * NY, -1) + jnp.roll(center, -2 * NY, -1)
    second = second + shift_columns(center, 2) + shift_columns(center, -2)
    return (potential_rows - potential_offset) * center - near_weight * nearest + far_weight * second


def chebyshev(start, potential):
    previous = start
    current = start
    for order in range(PASSES):
        extended = jnp.pad(current, ((0, 0), (2, 2), (0, 0)))
        operated = shifted_operator(extended, potential)
        if order == 0:
            following = operated / half_range
        else:
            following = (2.0 / half_range) * operated - previous
        previous, current = current, following
    return current


def reference(orbitals, rotation, potential):
    flattened = orbitals.reshape(NB, NZ * NXY)
    column_blocks = rotation.reshape(NB, NB // block_width, block_width).transpose(1, 0, 2)

    def filter_block(column_block):
        rotated = lax.dot_general(column_block, flattened, (((0,), (0,)), ((), ())), preferred_element_type=jnp.float32)
        rotated = rotated.astype(jnp.bfloat16).reshape(block_width, NZ, NXY)
        return chebyshev(rotated.astype(jnp.float32), potential)

    stacked = lax.map(filter_block, column_blocks)
    return stacked.reshape(NB, NZ, NXY)
```

```python
import functools

import jax
import jax.numpy as jnp
import numpy as np
from jax import lax
from jax.experimental import pallas as pl
from jax.experimental.pallas import tpu as pltpu
from jax.sharding import PartitionSpec as P

NY = 80
NXY = 3200
MESH = pl.DeviceIdType.MESH
F32 = jnp.float32
BF16 = jnp.bfloat16

potential_offset = 0.5
near_weight = 2.0 / 3.0
half_range = 4.25

TILES = 13
LANES = 128
SHARE = 200
WIDE = 3328
RING = 256 + WIDE + 256


def target_domain(h, y, z, c, half):
    return lax.rem(h + half, 2) * 8 + lax.rem(z + y + c + 2 * half, 4) * 2 + half


def place():
    band, dom = lax.axis_index("band"), lax.axis_index("dom")
    return band, dom, band // 4, lax.rem(band, 4), dom // 8, lax.rem(dom // 2, 4), lax.rem(dom, 2)


def exchange_kernel(
    orb_ref, rot_ref, pot_ref,
    own_ref, low_ref, high_ref, plow_ref, phigh_ref,
    head, tail, send1, recv1, send2, weights,
    s1, r1, s2, r2, sh, rh, sp, rp, ls,
):
    band, dom, h, y, x, z, c = place()
    mirror = (1 - x) * 8 + z * 2 + c
    has_low, has_high = dom > 0, dom < 15

    def partner(k):
        return lax.rem(h + k // 4, 2), lax.rem(y + lax.rem(k, 4), 4)

    barrier = pltpu.get_barrier_semaphore()

    def greet(b, d):
        pl.semaphore_signal(barrier, inc=1, device_id={"band": b, "dom": d}, device_id_type=MESH)

    for k in range(8):
        hh, yy = partner(k)
        greet(hh * 4 + yy, mirror)
    for half in range(2):
        for k in range(8):
            hh, yy = partner(k)
            greet(hh * 4 + yy, target_domain(h, y, z, c, half))
    for q in range(16):
        qz, qc = (q // 2) % 4, q % 2
        greet(lax.rem(x + c, 2) * 4 + lax.rem(z - qz - qc - 2 * c + 16, 4), q)
    up, down = lax.rem(dom + 1, 16), lax.rem(dom + 15, 16)
    greet(band, up)
    greet(band, down)

    def widen(o, _):
        rows = pl.ds(pl.multiple_of(o * 128, 128), 128)
        v = orb_ref[o].astype(F32)
        head[rows, :] = v[:, :LANES]
        tail[rows, :] = jnp.concatenate([v[:, LANES:], v[:, : 2 * LANES - SHARE]], axis=1)
        return 0

    lax.fori_loop(0, 24, widen, 0)

    lane = lax.broadcasted_iota(jnp.int32, (24, LANES), 1)
    turn = lax.rem(dom * 72, 128)
    r = rot_ref[...].astype(F32)
    r_left = r[:, :LANES]
    r_right = jnp.concatenate([r[:, LANES:], r[:, : 2 * LANES - 192]], axis=1)

    pl.semaphore_wait(barrier, 42)

    pot_copies = []
    for i, (dst, to, ok) in enumerate(((plow_ref, up, has_high), (phigh_ref, down, has_low))):
        cp = pltpu.make_async_remote_copy(
            src_ref=pot_ref, dst_ref=dst, send_sem=sp.at[i], recv_sem=rp.at[i],
            device_id={"band": band, "dom": to}, device_id_type=MESH)
        pot_copies.append(cp)
        pl.when(ok)(cp.start)

    def copy1(slot, source, to):
        return pltpu.make_async_remote_copy(
            src_ref=send1.at[slot], dst_ref=recv1.at[source], send_sem=s1.at[slot], recv_sem=r1.at[source],
            device_id={"band": to, "dom": mirror}, device_id_type=MESH)

    def pack(k, _):
        hh, yy = partner(k)
        parts = []
        for half in range(2):
            first = target_domain(hh, yy, z, c, half) * 8
            tiles = []
            for zz in range(8):
                v = head[pl.ds(first + zz, 24, stride=128), :]
                tiles.append(pltpu.roll(v, turn, 1))
            ends = [tail[pl.ds(first + zz, 24, stride=128), :] for zz in range(8)]
            for zz in range(4):
                v = jnp.where(lane < 64, ends[zz], pltpu.roll(ends[zz + 4], 64, 1))
                tiles.append(pltpu.roll(v, turn, 1))
            v = ends[0]
            for zz in range(1, 8):
                v = jnp.where(lane < 64 + 8 * zz, v, pltpu.roll(ends[zz], 8 * zz, 1))
            tiles.append(pltpu.roll(v, turn, 1))
            parts.append(tiles)
        parts[0].append(r_left)
        parts[1].append(r_right)
        for t in range(TILES + 1):
            a, b = parts[0][t], parts[1][t]
            send1[k, t, 0] = a[:16].astype(BF16)
            send1[k, t, 1] = b[:16].astype(BF16)
            send1[k, t, 2] = jnp.concatenate([a[16:], b[16:]], axis=0).astype(BF16)
        copy1(k, band, hh * 4 + yy).start()
        return 0

    lax.fori_loop(0, 8, pack, 0)
    for k in range(8):
        copy1(k, k, band).wait_recv()

    zero = jnp.zeros((8, 2 * LANES), F32)
    first_rows = jnp.concatenate([
        recv1[:, TILES, 0].astype(F32).reshape(128, LANES),
        recv1[:, TILES, 1].astype(F32).reshape(128, LANES)], axis=1)
    for half in range(2):
        rows = [first_rows]
        for k in range(8):
            m = recv1[k, TILES, 2].astype(F32)
            m = jnp.concatenate([m[:8], m[8:]], axis=1)
            rows += [m, zero] if half == 0 else [zero, m]
        weights[half] = jnp.transpose(jnp.concatenate(rows, axis=0))[:192].astype(BF16)

    lane8 = lax.broadcasted_iota(jnp.int32, (8, LANES), 1)
    in_window = lax.rem(lane8 - lax.rem(mirror * 72, 128) + 64 + 128, 128) < 64

    def copy2(slot, source, b, d):
        return pltpu.make_async_remote_copy(
            src_ref=send2.at[slot], dst_ref=own_ref.at[source], send_sem=s2.at[slot], recv_sem=r2.at[source],
            device_id={"band": b, "dom": d}, device_id_type=MESH)

    self_sent = False
    for half in range(2):
        def rhs(t):
            return jnp.concatenate(
                [recv1[:, t, half].reshape(128, LANES), recv1[:, t, 2].reshape(128, LANES)], axis=0)

        def pair(i, _):
            both = jnp.concatenate([rhs(2 * i), rhs(2 * i + 1)], axis=1)
            out = jnp.dot(weights[half], both, preferred_element_type=F32)
            for b in range(8):
                for g in range(3):
                    v = out[24 * b + 8 * g : 24 * b + 8 * g + 8]
                    v = jnp.concatenate([v[:, :LANES], v[:, LANES:]], axis=0)
                    send2[half * 8 + b, 6 * g + i] = v.astype(BF16)
            return 0

        lax.fori_loop(0, 6, pair, 0)
        out = jnp.dot(weights[half], rhs(12), preferred_element_type=F32)
        for b in range(8):
            v = out[24 * b : 24 * b + 24]
            first = jnp.where(in_window, v[:8], pltpu.roll(v[16:], 64, 1))
            send2[half * 8 + b, 18] = jnp.concatenate([first, v[8:16]], axis=0).astype(BF16)
        to_dom = target_domain(h, y, z, c, half)
        is_self = to_dom == dom
        self_sent = jnp.logical_or(self_sent, is_self)

        def post(k, _):
            hh, yy = partner(k)
            to = hh * 4 + yy
            here = jnp.logical_and(is_self, k == 0)

            @pl.when(jnp.logical_not(here))
            def _():
                copy2(half * 8 + to, mirror, to, to_dom).start()

            @pl.when(here)
            def _():
                pltpu.make_async_copy(send2.at[half * 8 + to], own_ref.at[mirror], ls).start()

            return 0

        lax.fori_loop(0, 8, post, 0)

    for q in range(16):
        here = jnp.logical_and(self_sent, mirror == q)

        @pl.when(jnp.logical_not(here))
        def _():
            copy2(q, q, band, dom).wait_recv()

        @pl.when(here)
        def _():
            pltpu.make_async_copy(send2.at[0], own_ref.at[q], ls).wait()

    halo = []
    for i, (dst, to, ok) in enumerate(((low_ref, up, has_high), (high_ref, down, has_low))):
        cp = pltpu.make_async_remote_copy(
            src_ref=own_ref, dst_ref=dst, send_sem=sh.at[i], recv_sem=rh.at[i],
            device_id={"band": band, "dom": to}, device_id_type=MESH)
        halo.append(cp)
        pl.when(ok)(cp.start)

    for k in range(8):
        copy1(k, k, band).wait_send()
    for half in range(2):
        is_self = target_domain(h, y, z, c, half) == dom
        for b in range(8):
            @pl.when(jnp.logical_not(jnp.logical_and(is_self, band == b)))
            def _():
                copy2(half * 8 + b, 0, band, dom).wait_send()
    for i, ok_send, ok_recv in ((0, has_high, has_low), (1, has_low, has_high)):
        pl.when(ok_send)(pot_copies[i].wait_send)
        pl.when(ok_recv)(pot_copies[i].wait_recv)
        pl.when(ok_send)(halo[i].wait_send)
        pl.when(ok_recv)(halo[i].wait_recv)


def neighbour_weights():
    out = np.zeros((5, 768, 256), np.float32)
    for w in range(5):
        for col in range(256):
            cell = 256 * w + col
            cy = cell % NY
            for step, value in ((1, 1.0), (2, -1.0 / 16.0)):
                for sign in (-1, 1):
                    out[w, col + 256 + sign * step * NY, col] += value
                    out[w, col + 256 + (cy + sign * step) % NY - cy, col] += value
    return out


def filter_kernel(
    own_ref, own_x, low_ref, low_x, high_ref, high_x, pot_ref, plow_ref, phigh_ref, w_ref,
    out_ref,
    even, odd, ring0, ring1, scaled, done,
):
    dom = lax.axis_index("dom")
    g = pl.program_id(0)
    inside = (dom > 0, None, dom < 15)
    lane = lax.broadcasted_iota(jnp.int32, (8, LANES), 1)

    @pl.when(g == 0)
    def _():
        for region, ref in enumerate((plow_ref, pot_ref, phigh_ref)):
            for zz in range(8):
                v = (ref[zz : zz + 1, :] - potential_offset) * (2.0 / half_range)
                if inside[region] is not None:
                    v = jnp.where(inside[region], v, 0.0)
                rows = pl.ds(64 * region + 8 * zz, 8)
                scaled[rows, :NXY] = jnp.broadcast_to(v, (8, NXY))
        scaled[:, NXY:] = jnp.zeros((192, WIDE - NXY), F32)
        even[:, NXY:] = jnp.zeros((192, WIDE - NXY), F32)
        odd[:, NXY:] = jnp.zeros((192, WIDE - NXY), F32)

    for region, (ref, xref) in enumerate(((low_ref, low_x), (own_ref, own_x), (high_ref, high_x))):
        last = []
        for d in range(16):
            v = xref[d, 0].astype(F32)
            v = jnp.where(g == 1, v[8:], v[:8])
            last.append(jnp.where(g == 2, pltpu.roll(v, 64, 1), v))
        for i in range(4):
            eights = []
            for zz in (2 * i, 2 * i + 1):
                v = None
                for d in range(16):
                    unit = (9 * d + 8 + zz) % 16
                    own = (lane // 8) == unit
                    v = last[d] if v is None else jnp.where(own, last[d], v)
                eights.append(pltpu.roll(v, (128 - 8 * zz) % 128, 1) if zz else v)
            pieces = [[] for _ in range(25)]
            for d in range(16):
                o, t0 = SHARE * d % 128, SHARE * d // 128
                hd = ref[d, i].astype(F32)
                pair = ((2 * i) % 4) // 2
                td = ref[d, 4 + pair].astype(F32)
                if i >= 2:
                    td = pltpu.roll(td, 64, 1)
                pieces[t0].append((o, 128, hd))
                if o:
                    pieces[t0 + 1].append((0, o, hd))
                end = o + 64
                pieces[t0 + 1].append((o, min(end, 128), td))
                if end > 128:
                    pieces[t0 + 2].append((0, end - 128, td))
                e = SHARE * d + 192
                pieces[e // 128].append((e % 128, e % 128 + 8, None))
            for t in range(25):
                ps = sorted(pieces[t], key=lambda p: p[0])
                assert ps[0][0] == 0 and ps[-1][1] == 128
                both = []
                for j in range(2):
                    v = None
                    for lo, hi, src in ps:
                        s = eights[j] if src is None else src[8 * j : 8 * j + 8]
                        v = s if v is None else jnp.where(lane < lo, v, s)
                    if inside[region] is not None:
                        v = jnp.where(inside[region], v, 0.0)
                    both.append(v)
                rows = slice(64 * region + 16 * i, 64 * region + 16 * i + 16)
                v = jnp.concatenate(both, axis=0)
                even[rows, 128 * t : 128 * t + 128] = v
                ring0[rows, 256 + 128 * t : 384 + 128 * t] = v.astype(BF16)

    def close(ring, first, last):
        rows = slice(8 * first, 8 * last)
        ring[rows, :256] = ring[rows, NXY : NXY + 256]
        ring[rows, 256 + NXY :] = ring[rows, 256 : 256 + RING - 256 - NXY]

    close(ring0, 0, 24)
    b_all = -near_weight * 2.0 / half_range
    b_low = jnp.where(inside[0], b_all, 0.0)
    b_high = jnp.where(inside[2], b_all, 0.0)
    rings = (ring0, ring1)
    for order in range(4):
        a, b = 2 * order + 2, 22 - 2 * order
        now, other = (even, odd) if order % 2 == 0 else (odd, even)
        ring, following = rings[order % 2], rings[(order + 1) % 2]

        def block(n, _):
            window = ring[8 * a : 8 * b, pl.ds(pl.multiple_of(256 * n, 256), 768)]
            planar = jnp.dot(window, w_ref[lax.rem(n, 5)], preferred_element_type=F32)
            for l in range(2):
                cols = pl.ds(pl.multiple_of(256 * n + 128 * l, 128), 128)
                v = [now[8 * q : 8 * q + 8, cols] for q in range(a - 2, b + 2)]
                pending = None
                for q in range(a, b):
                    m = q - a + 2
                    near = v[m - 1] + v[m + 1]
                    far = v[m - 2] + v[m + 2]
                    t = planar[8 * (q - a) : 8 * (q - a) + 8, 128 * l : 128 * l + 128] + near - far * (1.0 / 16.0)
                    coef = b_low if q < 8 else (b_all if q < 16 else b_high)
                    new = scaled[8 * q : 8 * q + 8, cols] * v[m] + coef * t
                    if order == 0:
                        new = new * 0.5
                    else:
                        new = new - other[8 * q : 8 * q + 8, cols]
                    if order < 3:
                        other[8 * q : 8 * q + 8, cols] = new
                        if q % 2 == 0:
                            pending = new
                        else:
                            ring_cols = pl.ds(pl.multiple_of(256 * n + 128 * l + 256, 128), 128)
                            following[8 * q - 8 : 8 * q + 8, ring_cols] = jnp.concatenate(
                                [pending, new], axis=0).astype(BF16)
                    else:
                        rows = pl.ds(pl.multiple_of(64 * (2 * n + l) + 8 * (q - 8), 8), 8)
                        done[rows, :] = new
            return 0

        lax.fori_loop(0, 13, block, 0)
        if order < 3:
            close(following, a, b)
    def turn_out(t, _):
        cols = pl.ds(pl.multiple_of(128 * t, 128), 128)
        for o in range(8):
            out_ref[8 * o : 8 * o + 8, cols] = done[pl.ds(64 * t + o, 8, stride=8), :]
        return 0

    lax.fori_loop(0, 25, turn_out, 0)


def body(orbitals, rotation, potential, weights):
    vmem = pl.BlockSpec(memory_space=pltpu.VMEM)
    anyspace = pl.BlockSpec(memory_space=pl.ANY)
    packed = jax.ShapeDtypeStruct((16, 19, 16, LANES), BF16)
    plane = jax.ShapeDtypeStruct((8, NXY), F32)
    own, low, high, plow, phigh = pl.pallas_call(
        exchange_kernel,
        out_shape=[packed, packed, packed, plane, plane],
        in_specs=[vmem, vmem, anyspace],
        out_specs=[anyspace] * 5,
        scratch_shapes=[
            pltpu.VMEM((24 * 128, LANES), F32),
            pltpu.VMEM((24 * 128, LANES), F32),
            pltpu.VMEM((8, TILES + 1, 3, 16, LANES), BF16),
            pltpu.VMEM((8, TILES + 1, 3, 16, LANES), BF16),
            pltpu.VMEM((16, 19, 16, LANES), BF16),
            pltpu.VMEM((2, 192, 256), BF16),
            pltpu.SemaphoreType.DMA((8,)),
            pltpu.SemaphoreType.DMA((8,)),
            pltpu.SemaphoreType.DMA((16,)),
            pltpu.SemaphoreType.DMA((16,)),
            pltpu.SemaphoreType.DMA((2,)),
            pltpu.SemaphoreType.DMA((2,)),
            pltpu.SemaphoreType.DMA((2,)),
            pltpu.SemaphoreType.DMA((2,)),
            pltpu.SemaphoreType.DMA,
        ],
        compiler_params=pltpu.CompilerParams(
            collective_id=0, has_side_effects=True, vmem_limit_bytes=40 << 20),
        name="exchange",
    )(orbitals, rotation, potential)

    blocks = pl.BlockSpec((16, 6, 16, LANES), lambda g: (0, g, 0, 0))
    lasts = pl.BlockSpec((16, 1, 16, LANES), lambda g: (0, 18, 0, 0))
    whole = pl.BlockSpec((8, NXY), lambda g: (0, 0))
    out = pl.pallas_call(
        filter_kernel,
        grid=(3,),
        out_shape=jax.ShapeDtypeStruct((192, NXY), F32),
        in_specs=[blocks, lasts, blocks, lasts, blocks, lasts, whole, whole, whole,
                  pl.BlockSpec((5, 768, 256), lambda g: (0, 0, 0))],
        out_specs=pl.BlockSpec((64, NXY), lambda g: (g, 0)),
        scratch_shapes=[
            pltpu.VMEM((192, WIDE), F32),
            pltpu.VMEM((192, WIDE), F32),
            pltpu.VMEM((192, RING), BF16),
            pltpu.VMEM((192, RING), BF16),
            pltpu.VMEM((192, WIDE), F32),
            pltpu.VMEM((WIDE // LANES * 64, LANES), F32),
        ],
        compiler_params=pltpu.CompilerParams(vmem_limit_bytes=48 << 20),
        name="filter",
    )(own, own, low, low, high, high, potential, plow, phigh, weights)
    return out.reshape(24, 8, NXY)


def solution(mesh):
    in_specs = (P("band", None, "dom"), P("band", None), P("dom", None), P())
    out_specs = P("band", "dom", None)
    run = jax.shard_map(body, mesh=mesh, in_specs=in_specs, out_specs=out_specs, check_vma=False)

    def whole(orbitals, rotation, potential):
        return run(orbitals, rotation, potential, jnp.asarray(neighbour_weights(), BF16))

    return whole
```

```python
import functools

import jax
import jax.numpy as jnp
import numpy as np
from jax import lax
from jax.experimental import pallas as pl
from jax.experimental.pallas import tpu as pltpu
from jax.sharding import PartitionSpec as P

NY = 80
NXY = 3200
MESH = pl.DeviceIdType.MESH
F32 = jnp.float32
BF16 = jnp.bfloat16

potential_offset = 0.5
near_weight = 2.0 / 3.0
half_range = 4.25

TILES = 13
LANES = 128
SHARE = 200
WIDE = 3328
RING = 256 + WIDE + 256


def target_domain(h, y, z, c, half):
    return lax.rem(h + half, 2) * 8 + lax.rem(z + y + c + 2 * half, 4) * 2 + half


def place():
    band, dom = lax.axis_index("band"), lax.axis_index("dom")
    return band, dom, band // 4, lax.rem(band, 4), dom // 8, lax.rem(dom // 2, 4), lax.rem(dom, 2)


def exchange_kernel(
    orb_ref, rot_ref, pot_ref,
    own_ref, low_ref, high_ref, plow_ref, phigh_ref,
    head, tail, send1, recv1, send2, weights,
    s1, r1, s2, r2, sh, rh, sp, rp, ls,
):
    band, dom, h, y, x, z, c = place()
    mirror = (1 - x) * 8 + z * 2 + c
    has_low, has_high = dom > 0, dom < 15

    def partner(k):
        return lax.rem(h + k // 4, 2), lax.rem(y + lax.rem(k, 4), 4)

    barrier = pltpu.get_barrier_semaphore()

    def greet(b, d):
        pl.semaphore_signal(barrier, inc=1, device_id={"band": b, "dom": d}, device_id_type=MESH)

    for k in range(8):
        hh, yy = partner(k)
        greet(hh * 4 + yy, mirror)
    for half in range(2):
        for k in range(8):
            hh, yy = partner(k)
            greet(hh * 4 + yy, target_domain(h, y, z, c, half))
    for q in range(16):
        qz, qc = (q // 2) % 4, q % 2
        greet(lax.rem(x + c, 2) * 4 + lax.rem(z - qz - qc - 2 * c + 16, 4), q)
    up, down = lax.rem(dom + 1, 16), lax.rem(dom + 15, 16)
    greet(band, up)
    greet(band, down)

    def widen(o, _):
        rows = pl.ds(pl.multiple_of(o * 128, 128), 128)
        v = orb_ref[o].astype(F32)
        head[rows, :] = v[:, :LANES]
        tail[rows, :] = jnp.concatenate([v[:, LANES:], v[:, : 2 * LANES - SHARE]], axis=1)
        return 0

    lax.fori_loop(0, 24, widen, 0)

    lane = lax.broadcasted_iota(jnp.int32, (24, LANES), 1)
    turn = lax.rem(dom * 72, 128)
    r = rot_ref[...].astype(F32)
    r_left = r[:, :LANES]
    r_right = jnp.concatenate([r[:, LANES:], r[:, : 2 * LANES - 192]], axis=1)

    pl.semaphore_wait(barrier, 42)

    pot_copies = []
    for i, (dst, to, ok) in enumerate(((plow_ref, up, has_high), (phigh_ref, down, has_low))):
        cp = pltpu.make_async_remote_copy(
            src_ref=pot_ref, dst_ref=dst, send_sem=sp.at[i], recv_sem=rp.at[i],
            device_id={"band": band, "dom": to}, device_id_type=MESH)
        pot_copies.append(cp)
        pl.when(ok)(cp.start)

    def copy1(slot, source, to):
        return pltpu.make_async_remote_copy(
            src_ref=send1.at[slot], dst_ref=recv1.at[source], send_sem=s1.at[slot], recv_sem=r1.at[source],
            device_id={"band": to, "dom": mirror}, device_id_type=MESH)

    def pack(k, _):
        hh, yy = partner(k)
        parts = []
        for half in range(2):
            first = target_domain(hh, yy, z, c, half) * 8
            tiles = []
            for zz in range(8):
                v = head[pl.ds(first + zz, 24, stride=128), :]
                tiles.append(pltpu.roll(v, turn, 1))
            ends = [tail[pl.ds(first + zz, 24, stride=128), :] for zz in range(8)]
            for zz in range(4):
                v = jnp.where(lane < 64, ends[zz], pltpu.roll(ends[zz + 4], 64, 1))
                tiles.append(pltpu.roll(v, turn, 1))
            v = ends[0]
            for zz in range(1, 8):
                v = jnp.where(lane < 64 + 8 * zz, v, pltpu.roll(ends[zz], 8 * zz, 1))
            tiles.append(pltpu.roll(v, turn, 1))
            parts.append(tiles)
        parts[0].append(r_left)
        parts[1].append(r_right)
        for t in range(TILES + 1):
            a, b = parts[0][t], parts[1][t]
            send1[k, t, 0] = a[:16].astype(BF16)
            send1[k, t, 1] = b[:16].astype(BF16)
            send1[k, t, 2] = jnp.concatenate([a[16:], b[16:]], axis=0).astype(BF16)
        return 0

    lax.fori_loop(0, 8, pack, 0)

    def post1(i, _):
        k = lax.rem(i, 8)
        part = pl.ds(2 * (i // 8), 2)
        hh, yy = partner(k)
        pltpu.make_async_remote_copy(
            src_ref=send1.at[k, part], dst_ref=recv1.at[band, part], send_sem=s1.at[k], recv_sem=r1.at[band],
            device_id={"band": hh * 4 + yy, "dom": mirror}, device_id_type=MESH).start()
        return 0

    lax.fori_loop(0, 56, post1, 0)
    for k in range(8):
        copy1(k, k, band).wait_recv()

    zero = jnp.zeros((8, 2 * LANES), F32)
    first_rows = jnp.concatenate([
        recv1[:, TILES, 0].astype(F32).reshape(128, LANES),
        recv1[:, TILES, 1].astype(F32).reshape(128, LANES)], axis=1)
    for half in range(2):
        rows = [first_rows]
        for k in range(8):
            m = recv1[k, TILES, 2].astype(F32)
            m = jnp.concatenate([m[:8], m[8:]], axis=1)
            rows += [m, zero] if half == 0 else [zero, m]
        weights[half] = jnp.transpose(jnp.concatenate(rows, axis=0))[:192].astype(BF16)

    lane8 = lax.broadcasted_iota(jnp.int32, (8, LANES), 1)
    in_window = lax.rem(lane8 - lax.rem(mirror * 72, 128) + 64 + 128, 128) < 64

    def copy2(slot, source, b, d):
        return pltpu.make_async_remote_copy(
            src_ref=send2.at[slot], dst_ref=own_ref.at[source], send_sem=s2.at[slot], recv_sem=r2.at[source],
            device_id={"band": b, "dom": d}, device_id_type=MESH)

    self_sent = False
    for half in range(2):
        def rhs(t):
            return jnp.concatenate(
                [recv1[:, t, half].reshape(128, LANES), recv1[:, t, 2].reshape(128, LANES)], axis=0)

        def pair(i, _):
            both = jnp.concatenate([rhs(2 * i), rhs(2 * i + 1)], axis=1)
            out = jnp.dot(weights[half], both, preferred_element_type=F32)
            for b in range(8):
                for g in range(3):
                    v = out[24 * b + 8 * g : 24 * b + 8 * g + 8]
                    v = jnp.concatenate([v[:, :LANES], v[:, LANES:]], axis=0)
                    send2[half * 8 + b, 6 * g + i] = v.astype(BF16)
            return 0

        lax.fori_loop(0, 6, pair, 0)
        out = jnp.dot(weights[half], rhs(12), preferred_element_type=F32)
        for b in range(8):
            v = out[24 * b : 24 * b + 24]
            first = jnp.where(in_window, v[:8], pltpu.roll(v[16:], 64, 1))
            send2[half * 8 + b, 18] = jnp.concatenate([first, v[8:16]], axis=0).astype(BF16)
        to_dom = target_domain(h, y, z, c, half)
        is_self = to_dom == dom
        self_sent = jnp.logical_or(self_sent, is_self)

        def post(k, _):
            hh, yy = partner(k)
            to = hh * 4 + yy
            here = jnp.logical_and(is_self, k == 0)

            @pl.when(jnp.logical_not(here))
            def _():
                copy2(half * 8 + to, mirror, to, to_dom).start()

            @pl.when(here)
            def _():
                pltpu.make_async_copy(send2.at[half * 8 + to], own_ref.at[mirror], ls).start()

            return 0

        lax.fori_loop(0, 8, post, 0)

    for q in range(16):
        here = jnp.logical_and(self_sent, mirror == q)

        @pl.when(jnp.logical_not(here))
        def _():
            copy2(q, q, band, dom).wait_recv()

        @pl.when(here)
        def _():
            pltpu.make_async_copy(send2.at[0], own_ref.at[q], ls).wait()

    halo = []
    for i, (dst, to, ok) in enumerate(((low_ref, up, has_high), (high_ref, down, has_low))):
        cp = pltpu.make_async_remote_copy(
            src_ref=own_ref, dst_ref=dst, send_sem=sh.at[i], recv_sem=rh.at[i],
            device_id={"band": band, "dom": to}, device_id_type=MESH)
        halo.append(cp)
        pl.when(ok)(cp.start)

    for k in range(8):
        copy1(k, k, band).wait_send()
    for half in range(2):
        is_self = target_domain(h, y, z, c, half) == dom
        for b in range(8):
            @pl.when(jnp.logical_not(jnp.logical_and(is_self, band == b)))
            def _():
                copy2(half * 8 + b, 0, band, dom).wait_send()
    for i, ok_send, ok_recv in ((0, has_high, has_low), (1, has_low, has_high)):
        pl.when(ok_send)(pot_copies[i].wait_send)
        pl.when(ok_recv)(pot_copies[i].wait_recv)
        pl.when(ok_send)(halo[i].wait_send)
        pl.when(ok_recv)(halo[i].wait_recv)


def neighbour_weights():
    out = np.zeros((5, 768, 256), np.float32)
    for w in range(5):
        for col in range(256):
            cell = 256 * w + col
            cy = cell % NY
            for step, value in ((1, 1.0), (2, -1.0 / 16.0)):
                for sign in (-1, 1):
                    out[w, col + 256 + sign * step * NY, col] += value
                    out[w, col + 256 + (cy + sign * step) % NY - cy, col] += value
    return out


def filter_kernel(
    own_ref, own_x, low_ref, low_x, high_ref, high_x, pot_ref, plow_ref, phigh_ref, w_ref,
    out_ref,
    even, odd, ring0, ring1, scaled, done,
):
    dom = lax.axis_index("dom")
    g = pl.program_id(0)
    inside = (dom > 0, None, dom < 15)
    lane = lax.broadcasted_iota(jnp.int32, (8, LANES), 1)

    @pl.when(g == 0)
    def _():
        for region, ref in enumerate((plow_ref, pot_ref, phigh_ref)):
            for zz in range(8):
                v = (ref[zz : zz + 1, :] - potential_offset) * (2.0 / half_range)
                if inside[region] is not None:
                    v = jnp.where(inside[region], v, 0.0)
                rows = pl.ds(64 * region + 8 * zz, 8)
                scaled[rows, :NXY] = jnp.broadcast_to(v, (8, NXY))
        scaled[:, NXY:] = jnp.zeros((192, WIDE - NXY), F32)
        even[:, NXY:] = jnp.zeros((192, WIDE - NXY), F32)
        odd[:, NXY:] = jnp.zeros((192, WIDE - NXY), F32)

    for region, (ref, xref) in enumerate(((low_ref, low_x), (own_ref, own_x), (high_ref, high_x))):
        last = []
        for d in range(16):
            v = xref[d, 0].astype(F32)
            v = jnp.where(g == 1, v[8:], v[:8])
            last.append(jnp.where(g == 2, pltpu.roll(v, 64, 1), v))
        for i in range(4):
            eights = []
            for zz in (2 * i, 2 * i + 1):
                v = None
                for d in range(16):
                    unit = (9 * d + 8 + zz) % 16
                    own = (lane // 8) == unit
                    v = last[d] if v is None else jnp.where(own, last[d], v)
                eights.append(pltpu.roll(v, (128 - 8 * zz) % 128, 1) if zz else v)
            pieces = [[] for _ in range(25)]
            for d in range(16):
                o, t0 = SHARE * d % 128, SHARE * d // 128
                hd = ref[d, i].astype(F32)
                pair = ((2 * i) % 4) // 2
                td = ref[d, 4 + pair].astype(F32)
                if i >= 2:
                    td = pltpu.roll(td, 64, 1)
                pieces[t0].append((o, 128, hd))
                if o:
                    pieces[t0 + 1].append((0, o, hd))
                end = o + 64
                pieces[t0 + 1].append((o, min(end, 128), td))
                if end > 128:
                    pieces[t0 + 2].append((0, end - 128, td))
                e = SHARE * d + 192
                pieces[e // 128].append((e % 128, e % 128 + 8, None))
            for t in range(25):
                ps = sorted(pieces[t], key=lambda p: p[0])
                assert ps[0][0] == 0 and ps[-1][1] == 128
                both = []
                for j in range(2):
                    v = None
                    for lo, hi, src in ps:
                        s = eights[j] if src is None else src[8 * j : 8 * j + 8]
                        v = s if v is None else jnp.where(lane < lo, v, s)
                    if inside[region] is not None:
                        v = jnp.where(inside[region], v, 0.0)
                    both.append(v)
                rows = slice(64 * region + 16 * i, 64 * region + 16 * i + 16)
                v = jnp.concatenate(both, axis=0)
                even[rows, 128 * t : 128 * t + 128] = v
                ring0[rows, 256 + 128 * t : 384 + 128 * t] = v.astype(BF16)

    def close(ring, first, last):
        rows = slice(8 * first, 8 * last)
        ring[rows, :256] = ring[rows, NXY : NXY + 256]
        ring[rows, 256 + NXY :] = ring[rows, 256 : 256 + RING - 256 - NXY]

    close(ring0, 0, 24)
    b_all = -near_weight * 2.0 / half_range
    b_low = jnp.where(inside[0], b_all, 0.0)
    b_high = jnp.where(inside[2], b_all, 0.0)
    rings = (ring0, ring1)
    for order in range(4):
        a, b = 2 * order + 2, 22 - 2 * order
        now, other = (even, odd) if order % 2 == 0 else (odd, even)
        ring, following = rings[order % 2], rings[(order + 1) % 2]

        def sweep(w, _, count):
            windows = [
                ring[8 * a : 8 * b, pl.ds(pl.multiple_of(256 * w + 1280 * i, 256), 768)] for i in range(count)]
            planar = jnp.dot(jnp.concatenate(windows, axis=0), w_ref[w], preferred_element_type=F32)
            for i in range(count):
                block(w + 5 * i, planar[8 * (b - a) * i : 8 * (b - a) * (i + 1)])
            return 0

        def block(n, planar):
            for l in range(2):
                cols = pl.ds(pl.multiple_of(256 * n + 128 * l, 128), 128)
                v = [now[8 * q : 8 * q + 8, cols] for q in range(a - 2, b + 2)]
                pending = None
                for q in range(a, b):
                    m = q - a + 2
                    near = v[m - 1] + v[m + 1]
                    far = v[m - 2] + v[m + 2]
                    t = planar[8 * (q - a) : 8 * (q - a) + 8, 128 * l : 128 * l + 128] + near - far * (1.0 / 16.0)
                    coef = b_low if q < 8 else (b_all if q < 16 else b_high)
                    new = scaled[8 * q : 8 * q + 8, cols] * v[m] + coef * t
                    if order == 0:
                        new = new * 0.5
                    else:
                        new = new - other[8 * q : 8 * q + 8, cols]
                    if order < 3:
                        other[8 * q : 8 * q + 8, cols] = new
                        if q % 2 == 0:
                            pending = new
                        else:
                            ring_cols = pl.ds(pl.multiple_of(256 * n + 128 * l + 256, 128), 128)
                            following[8 * q - 8 : 8 * q + 8, ring_cols] = jnp.concatenate(
                                [pending, new], axis=0).astype(BF16)
                    else:
                        rows = pl.ds(pl.multiple_of(64 * (2 * n + l) + 8 * (q - 8), 8), 8)
                        done[rows, :] = new

        lax.fori_loop(0, 3, functools.partial(sweep, count=3), 0)
        lax.fori_loop(3, 5, functools.partial(sweep, count=2), 0)
        if order < 3:
            close(following, a, b)
    def turn_out(t, _):
        cols = pl.ds(pl.multiple_of(128 * t, 128), 128)
        for o in range(8):
            out_ref[8 * o : 8 * o + 8, cols] = done[pl.ds(64 * t + o, 8, stride=8), :]
        return 0

    lax.fori_loop(0, 25, turn_out, 0)


def body(orbitals, rotation, potential, weights):
    vmem = pl.BlockSpec(memory_space=pltpu.VMEM)
    anyspace = pl.BlockSpec(memory_space=pl.ANY)
    packed = jax.ShapeDtypeStruct((16, 19, 16, LANES), BF16)
    plane = jax.ShapeDtypeStruct((8, NXY), F32)
    own, low, high, plow, phigh = pl.pallas_call(
        exchange_kernel,
        out_shape=[packed, packed, packed, plane, plane],
        in_specs=[vmem, vmem, anyspace],
        out_specs=[anyspace] * 5,
        scratch_shapes=[
            pltpu.VMEM((24 * 128, LANES), F32),
            pltpu.VMEM((24 * 128, LANES), F32),
            pltpu.VMEM((8, TILES + 1, 3, 16, LANES), BF16),
            pltpu.VMEM((8, TILES + 1, 3, 16, LANES), BF16),
            pltpu.VMEM((16, 19, 16, LANES), BF16),
            pltpu.VMEM((2, 192, 256), BF16),
            pltpu.SemaphoreType.DMA((8,)),
            pltpu.SemaphoreType.DMA((8,)),
            pltpu.SemaphoreType.DMA((16,)),
            pltpu.SemaphoreType.DMA((16,)),
            pltpu.SemaphoreType.DMA((2,)),
            pltpu.SemaphoreType.DMA((2,)),
            pltpu.SemaphoreType.DMA((2,)),
            pltpu.SemaphoreType.DMA((2,)),
            pltpu.SemaphoreType.DMA,
        ],
        compiler_params=pltpu.CompilerParams(
            collective_id=0, has_side_effects=True, vmem_limit_bytes=40 << 20),
        name="exchange",
    )(orbitals, rotation, potential)

    blocks = pl.BlockSpec((16, 6, 16, LANES), lambda g: (0, g, 0, 0))
    lasts = pl.BlockSpec((16, 1, 16, LANES), lambda g: (0, 18, 0, 0))
    whole = pl.BlockSpec((8, NXY), lambda g: (0, 0))
    out = pl.pallas_call(
        filter_kernel,
        grid=(3,),
        out_shape=jax.ShapeDtypeStruct((192, NXY), F32),
        in_specs=[blocks, lasts, blocks, lasts, blocks, lasts, whole, whole, whole,
                  pl.BlockSpec((5, 768, 256), lambda g: (0, 0, 0))],
        out_specs=pl.BlockSpec((64, NXY), lambda g: (g, 0)),
        scratch_shapes=[
            pltpu.VMEM((192, WIDE), F32),
            pltpu.VMEM((192, WIDE), F32),
            pltpu.VMEM((192, RING), BF16),
            pltpu.VMEM((192, RING), BF16),
            pltpu.VMEM((192, WIDE), F32),
            pltpu.VMEM((WIDE // LANES * 64, LANES), F32),
        ],
        compiler_params=pltpu.CompilerParams(vmem_limit_bytes=48 << 20),
        name="filter",
    )(own, own, low, low, high, high, potential, plow, phigh, weights)
    return out.reshape(24, 8, NXY)


def solution(mesh):
    in_specs = (P("band", None, "dom"), P("band", None), P("dom", None), P())
    out_specs = P("band", "dom", None)
    run = jax.shard_map(body, mesh=mesh, in_specs=in_specs, out_specs=out_specs, check_vma=False)

    def whole(orbitals, rotation, potential):
        return run(orbitals, rotation, potential, jnp.asarray(neighbour_weights(), BF16))

    return whole
```

```python
import jax
import jax.numpy as jnp
import numpy as np
from jax import lax
from jax.experimental import pallas as pl
from jax.experimental.pallas import tpu as pltpu
from jax.sharding import PartitionSpec as P

NXY = 3200
MESH = pl.DeviceIdType.MESH
F32 = jnp.float32
BF16 = jnp.bfloat16
LANES = 128

potential_offset = 0.5
near_weight = 2.0 / 3.0
half_range = 4.25


def target_domain(h, y, z, c, half):
    return lax.rem(h + half, 2) * 8 + lax.rem(z + y + c + 2 * half, 4) * 2 + half


def kernel(
    orb_hbm, rot_hbm, pot_hbm, wy_ref,
    out_hbm,
    orb, rot, pot, wide, send1, recv1, send2, weights,
    own, low, high, pown, plow, phigh,
    even, odd, ring0, ring1, scaled, done, result,
    s1, r1, s2, r2, sh, rh, sp, rp, ls, li, lo,
):
    band, dom = lax.axis_index("band"), lax.axis_index("dom")
    h, y = band // 4, lax.rem(band, 4)
    x, z, c = dom // 8, lax.rem(dom // 2, 4), lax.rem(dom, 2)
    mirror = (1 - x) * 8 + z * 2 + c
    has_low, has_high = dom > 0, dom < 15
    up, down = lax.rem(dom + 1, 16), lax.rem(dom + 15, 16)

    def partner(k):
        return lax.rem(h + k // 4, 2) * 4 + lax.rem(y + lax.rem(k, 4), 4)

    def load(i):
        return pltpu.make_async_copy(orb_hbm.at[pl.ds(4 * i, 4)], orb.at[pl.ds(4 * i, 4)], li.at[i])

    load_rot = pltpu.make_async_copy(rot_hbm, rot, li.at[6])
    load_pot = pltpu.make_async_copy(pot_hbm, pot, li.at[7])
    for i in range(6):
        load(i).start()
    load_rot.start()
    load_pot.start()

    barrier = pltpu.get_barrier_semaphore()

    def greet(b, d):
        pl.semaphore_signal(barrier, inc=1, device_id={"band": b, "dom": d}, device_id_type=MESH)

    greet(band, up)
    greet(band, down)
    lane = lax.broadcasted_iota(jnp.int32, (8, LANES), 1)
    block = lane // 16
    lane24 = lax.broadcasted_iota(jnp.int32, (24, LANES), 1)
    block24 = lane24 // 16

    for i in range(6):
        load(i).wait()

        def widen(o, _):
            k = lax.rem(o, 8)
            half = jnp.where(o < 16, 0, 1)
            greet(partner(k), jnp.where(o < 8, mirror, target_domain(h, y, z, c, half)))

            @pl.when(o < 16)
            def _():
                qz, qc = lax.rem(o // 2, 4), lax.rem(o, 2)
                greet(lax.rem(x + c, 2) * 4 + lax.rem(z - qz - qc - 2 * c + 16, 4), o)

            rows = pl.ds(pl.multiple_of(o * 128, 128), 128)
            v = orb[o].astype(F32)
            a, b = v[:, :LANES], jnp.concatenate([v[:, LANES:], v[:, : 256 - 200]], axis=1)
            wide[0, rows, :] = jnp.where(c == 0, a, jnp.concatenate([v[:, 8:128], v[:, 128:136]], axis=1))
            wide[1, rows, :] = jnp.where(
                c == 0, b, jnp.concatenate([v[:, 136:200], v[:, : 128 - 64]], axis=1))
            return 0

        lax.fori_loop(4 * i, 4 * i + 4, widen, 0)

    load_rot.wait()
    r = rot[...].astype(F32)
    r_left = r[:, :LANES]
    r_right = jnp.concatenate([r[:, LANES:], r[:, : 256 - 192]], axis=1)

    def pack(t, u, half, k, own_turn):
        to = partner(k)
        first = target_domain(to // 4, lax.rem(to, 4), z, c, half) * 8
        v = None
        for zz in range(8):
            s = pltpu.roll(wide[u // 8, pl.ds(first + zz, 24, stride=128), :], 16 * zz, 1)
            v = s if v is None else jnp.where(block24 == lax.rem(u + zz, 8), s, v)
        return pltpu.roll(v, own_turn, 1)

    def put(k, t, a, b):
        send1[k, t, 0] = a[:16].astype(BF16)
        send1[k, t, 1] = b[:16].astype(BF16)
        send1[k, t, 2] = jnp.concatenate([a[16:], b[16:]], axis=0).astype(BF16)

    def copy1(slot, source, part, to):
        rows = pl.ds(2 * part, 2)
        return pltpu.make_async_remote_copy(
            src_ref=send1.at[slot, rows], dst_ref=recv1.at[source, rows],
            send_sem=s1.at[part, slot], recv_sem=r1.at[part, source],
            device_id={"band": to, "dom": mirror}, device_id_type=MESH)

    turn = (dom // 2) * 16
    pl.semaphore_wait(barrier, 42)

    def ends(k, _):
        put(k, 0, *[pack(0, 12, half, k, turn + 8 * c) for half in range(2)])
        put(k, 1, r_left, r_right)
        copy1(k, band, 0, partner(k)).start()
        return 0

    lax.fori_loop(0, 8, ends, 0)

    def units(i, _):
        part, k = i // 8 + 1, lax.rem(i, 8)
        for j in range(2):
            u = 2 * part - 2 + j
            put(k, u + 2, *[pack(u + 2, u, half, k, turn) for half in range(2)])
        copy1(k, band, part, partner(k)).start()
        return 0

    lax.fori_loop(0, 48, units, 0)

    load_pot.wait()
    for t in range(25):
        v = None
        for p in range(8):
            tile = (25 * p + t) // 8
            s = pot[:, 128 * tile : 128 * tile + 128]
            v = s if v is None else jnp.where(block == (p + t) % 8, s, v)
        if t % 8:
            v = pltpu.roll(v, 128 - 16 * (t % 8), 1)
        pown[t] = (v - potential_offset) * (2.0 / half_range)

    pot_copies = []
    for i, (dst, to, ok) in enumerate(((plow, up, has_high), (phigh, down, has_low))):
        cp = pltpu.make_async_remote_copy(
            src_ref=pown, dst_ref=dst, send_sem=sp.at[i], recv_sem=rp.at[i],
            device_id={"band": band, "dom": to}, device_id_type=MESH)
        pot_copies.append(cp)
        pl.when(ok)(cp.start)

    for k in range(8):
        copy1(k, k, 0, band).wait_recv()
    zero = jnp.zeros((8, 2 * LANES), F32)
    first_rows = jnp.concatenate([
        recv1[:, 1, 0].astype(F32).reshape(128, LANES),
        recv1[:, 1, 1].astype(F32).reshape(128, LANES)], axis=1)
    for half in range(2):
        rows = [first_rows]
        for k in range(8):
            m = recv1[k, 1, 2].astype(F32)
            m = jnp.concatenate([m[:8], m[8:]], axis=1)
            rows += [m, zero] if half == 0 else [zero, m]
        weights[half] = jnp.transpose(jnp.concatenate(rows, axis=0))[:192].astype(BF16)

    def rhs(t, half):
        return jnp.concatenate(
            [recv1[:, t, half].reshape(128, LANES), recv1[:, t, 2].reshape(128, LANES)], axis=0)

    is_odd_half = lax.rem(lane // 8, 2)
    for half in range(2):
        out = jnp.dot(weights[half], rhs(0, half), preferred_element_type=F32)
        for b in range(8):
            v = out[24 * b : 24 * b + 24]
            first = jnp.where(is_odd_half == c, v[:8], pltpu.roll(v[16:], jnp.where(c == 0, 8, 120), 1))
            send2[half * 8 + b, 0, 6] = jnp.concatenate([first, v[8:16]], axis=0).astype(BF16)

    def rotate(part, _):
        for k in range(8):
            copy1(k, k, part, band).wait_recv()
        for half in range(2):
            both = jnp.concatenate([rhs(2 * part, half), rhs(2 * part + 1, half)], axis=1)
            out = jnp.dot(weights[half], both, preferred_element_type=F32)
            for b in range(8):
                for g in range(3):
                    v = out[24 * b + 8 * g : 24 * b + 8 * g + 8]
                    v = jnp.concatenate([v[:, :LANES], v[:, LANES:]], axis=0)
                    send2[half * 8 + b, g, part - 1] = v.astype(BF16)
        return 0

    lax.fori_loop(1, 7, rotate, 0)

    def tiles(g):
        return pl.ds(0, 7 if g == 0 else 6)

    def copy2(slot, source, g, b, d):
        return pltpu.make_async_remote_copy(
            src_ref=send2.at[slot, g, tiles(g)], dst_ref=own.at[g, source, tiles(g)],
            send_sem=s2.at[g, slot], recv_sem=r2.at[g, source],
            device_id={"band": b, "dom": d}, device_id_type=MESH)

    def keep(slot, source, g):
        return pltpu.make_async_copy(send2.at[slot, g, tiles(g)], own.at[g, source, tiles(g)], ls.at[g])

    def is_self(half):
        return target_domain(h, y, z, c, half) == dom

    for g in range(3):
        def post(i, _):
            half, k = i // 8, lax.rem(i, 8)
            to, to_dom = partner(k), target_domain(h, y, z, c, half)
            here = jnp.logical_and(to_dom == dom, k == 0)

            @pl.when(jnp.logical_not(here))
            def _():
                copy2(half * 8 + to, mirror, g, to, to_dom).start()

            @pl.when(here)
            def _():
                keep(half * 8 + to, mirror, g).start()

            return 0

        lax.fori_loop(0, 16, post, 0)

    self_sent = jnp.logical_or(is_self(0), is_self(1))

    def halo(i, g):
        dst, to = ((low, up), (high, down))[i]
        return pltpu.make_async_remote_copy(
            src_ref=own.at[g, :, tiles(g)], dst_ref=dst.at[g, :, tiles(g)], send_sem=sh.at[i, g], recv_sem=rh.at[i, g],
            device_id={"band": band, "dom": to}, device_id_type=MESH)

    def arrive(g):
        def one(q, _):
            here = jnp.logical_and(self_sent, mirror == q)

            @pl.when(jnp.logical_not(here))
            def _():
                copy2(q, q, g, band, dom).wait_recv()

            @pl.when(here)
            def _():
                keep(0, q, g).wait()

            return 0

        lax.fori_loop(0, 16, one, 0)
        pl.when(has_high)(halo(0, g).start)
        pl.when(has_low)(halo(1, g).start)

    inside = (has_low, None, has_high)
    for i, ok_send, ok_recv in ((0, has_high, has_low), (1, has_low, has_high)):
        pl.when(ok_recv)(pot_copies[i].wait_recv)

    for region, ref in enumerate((plow, pown, phigh)):
        def spread(t, _):
            v = ref[t]
            if inside[region] is not None:
                v = jnp.where(inside[region], v, 0.0)
            for zz in range(8):
                rows = slice(64 * region + 8 * zz, 64 * region + 8 * zz + 8)
                scaled[t, rows, :] = jnp.broadcast_to(v[zz : zz + 1], (8, LANES))
            return 0

        lax.fori_loop(0, 25, spread, 0)

    b_all = -near_weight * 2.0 / half_range
    b_low = jnp.where(has_low, b_all, 0.0)
    b_high = jnp.where(has_high, b_all, 0.0)
    rings = (ring0, ring1)

    def to_ring(ring, t, rows, v):
        xl, yh = t // 5, t % 5
        for pos in {0: (1, 6), 1: (2, 7), 4: (5, 0)}.get(yh, (yh + 1,)):
            ring[xl, rows, 128 * pos : 128 * pos + 128] = v

    def unpack(region, ref, g):
        def finish(t, zz, pair):
            if inside[region] is not None:
                pair = [jnp.where(inside[region], v, 0.0) for v in pair]
            v = jnp.concatenate(pair, axis=0)
            rows = slice(64 * region + 8 * zz, 64 * region + 8 * zz + 16)
            even[t, rows, :] = v
            to_ring(ring0, t, rows, v.astype(BF16))

        for e in range(2):
            for i in range(6):
                src = [ref[g, 2 * p + e, i].astype(F32) for p in range(8)]
                for j in range(2):
                    u = 2 * i + j
                    for zz in range(0, 8, 2):
                        pair = []
                        for s in (u + zz, u + zz + 1):
                            v = src[0][8 * j : 8 * j + 8]
                            for p in range(1, 8):
                                v = jnp.where(block == (s + p) % 8, src[p][8 * j : 8 * j + 8], v)
                            pair.append(pltpu.roll(v, 128 - 16 * (s % 8), 1) if s % 8 else v)
                        finish(13 * e + u, zz, pair)
        src = []
        for d in range(16):
            v = ref[0, d, 6].astype(F32)
            v = jnp.where(g == 1, v[8:], v[:8])
            src.append(jnp.where(g == 2, pltpu.roll(v, 8 if d % 2 else 120, 1), v))
        for zz in range(0, 8, 2):
            pair = []
            for s in (12 + zz, 13 + zz):
                v = src[0]
                for d in range(1, 16):
                    v = jnp.where(lane // 8 == 2 * ((s + d // 2) % 8) + d % 2, src[d], v)
                pair.append(pltpu.roll(v, 128 - 16 * (s % 8), 1) if s % 8 else v)
            finish(12, zz, pair)

    def step(order):
        a, b = 2 * order + 2, 22 - 2 * order
        now, other = (even, odd) if order % 2 == 0 else (odd, even)
        ring, following = rings[order % 2], rings[(order + 1) % 2]
        count = 8 * (b - a)
        for n in range(3):
            window = jnp.concatenate(
                [ring[xl, 8 * a : 8 * b, 256 * n : 256 * n + 512] for xl in range(5)], axis=0)
            width = 256 if n < 2 else 128
            planar = jnp.dot(window, wy_ref[:, :width], preferred_element_type=F32)
            for l in range(width // 128):
                yh = 2 * n + l
                v = {q: [now[5 * xl + yh, 8 * q : 8 * q + 8, :] for xl in range(5)] for q in range(a - 2, b + 2)}
                pending = None
                for q in range(a, b):
                    m = v[q]
                    before = [pltpu.roll(m[3], 16, 1), pltpu.roll(m[4], 16, 1)]
                    after = [pltpu.roll(m[0], 112, 1), pltpu.roll(m[1], 112, 1)]
                    line = before + m + after
                    coef = b_low if q < 8 else (b_all if q < 16 else b_high)
                    news = []
                    for xl in range(5):
                        t = 5 * xl + yh
                        near = (line[xl + 1] + line[xl + 3]) + (v[q - 1][xl] + v[q + 1][xl])
                        far = (line[xl] + line[xl + 4]) + (v[q - 2][xl] + v[q + 2][xl])
                        rows = slice(8 * q, 8 * q + 8)
                        first = count * xl + 8 * (q - a)
                        total = planar[first : first + 8, 128 * l : 128 * l + 128] + near - far * (1.0 / 16.0)
                        new = scaled[t, rows, :] * m[xl] + coef * total
                        if order == 0:
                            new = new * 0.5
                        else:
                            new = new - other[t, rows, :]
                        if order < 3:
                            other[t, rows, :] = new
                        else:
                            done[64 * t + 8 * (q - 8) : 64 * t + 8 * (q - 8) + 8, :] = new
                        news.append(new)
                    if order < 3:
                        if q % 2:
                            for xl in range(5):
                                to_ring(following, 5 * xl + yh, slice(8 * q - 8, 8 * q + 8),
                                        jnp.concatenate([pending[xl], news[xl]], axis=0).astype(BF16))
                        pending = news

    def write(g):
        return pltpu.make_async_copy(result.at[g], out_hbm.at[pl.ds(pl.multiple_of(64 * g, 64), 64)], lo.at[g])

    arrive(0)

    def group(g, _):
        for nxt in (1, 2):
            @pl.when(g == nxt - 1)
            def _():
                arrive(nxt)

        for now in range(3):
            @pl.when(g == now)
            def _():
                pl.when(has_low)(halo(0, now).wait_recv)
                pl.when(has_high)(halo(1, now).wait_recv)

        for region, ref in enumerate((low, own, high)):
            unpack(region, ref, g)
        for order in range(4):
            step(order)

        def turn_out(o, _):
            v = []
            for t in range(25):
                s = done[pl.ds(64 * t + o, 8, stride=8), :]
                v.append(pltpu.roll(s, 16 * (t % 8), 1) if t % 8 else s)
            rows = pl.ds(pl.multiple_of(8 * o, 8), 8)
            for tau in range(25):
                s = v[8 * tau % 25]
                for beta in range(1, 8):
                    s = jnp.where(block == beta, v[(8 * tau + beta) % 25], s)
                result[g, rows, 128 * tau : 128 * tau + 128] = s
            return 0

        lax.fori_loop(0, 8, turn_out, 0)
        write(g).start()
        return 0

    lax.fori_loop(0, 3, group, 0)

    def drain1(i, _):
        copy1(lax.rem(i, 8), 0, i // 8, band).wait_send()
        return 0

    lax.fori_loop(0, 56, drain1, 0)
    for g in range(3):
        def drain2(slot, _):
            here = jnp.logical_and(target_domain(h, y, z, c, slot // 8) == dom, lax.rem(slot, 8) == band)

            @pl.when(jnp.logical_not(here))
            def _():
                copy2(slot, 0, g, band, dom).wait_send()

            return 0

        lax.fori_loop(0, 16, drain2, 0)
        pl.when(has_high)(halo(0, g).wait_send)
        pl.when(has_low)(halo(1, g).wait_send)
    pl.when(has_high)(pot_copies[0].wait_send)
    pl.when(has_low)(pot_copies[1].wait_send)
    for g in range(3):
        write(g).wait()


def y_weights():
    out = np.zeros((512, 256), np.float32)
    for col in range(256):
        j, p, yl = col // 128, col % 128 // 16, col % 16
        for step, value in ((1, 1.0), (2, -1.0 / 16.0)):
            for sign in (-1, 1):
                at = yl + sign * step
                out[128 * (1 + j + at // 16) + 16 * p + at % 16, col] += value
    return out


def body(orbitals, rotation, potential, weights):
    anyspace = pl.BlockSpec(memory_space=pl.ANY)
    dma = pltpu.SemaphoreType.DMA
    group = pltpu.VMEM((3, 16, 7, 16, LANES), BF16)
    plane = pltpu.VMEM((25, 8, LANES), F32)
    field = pltpu.VMEM((25, 192, LANES), F32)
    ring = pltpu.VMEM((5, 192, 1024), BF16)
    parts = pltpu.VMEM((8, 14, 3, 16, LANES), BF16)
    out = pl.pallas_call(
        kernel,
        out_shape=jax.ShapeDtypeStruct((192, NXY), F32),
        in_specs=[anyspace, anyspace, anyspace, pl.BlockSpec(memory_space=pltpu.VMEM)],
        out_specs=anyspace,
        scratch_shapes=[
            pltpu.VMEM((24, 128, 200), BF16),
            pltpu.VMEM((24, 192), BF16),
            pltpu.VMEM((8, NXY), F32),
            pltpu.VMEM((2, 24 * 128, LANES), F32),
            parts, parts,
            pltpu.VMEM((16, 3, 7, 16, LANES), BF16),
            pltpu.VMEM((2, 192, 256), BF16),
            group, group, group,
            plane, plane, plane,
            field, field, ring, ring, field,
            pltpu.VMEM((25 * 64, LANES), F32),
            pltpu.VMEM((3, 64, NXY), F32),
            dma((7, 8)), dma((7, 8)), dma((3, 16)), dma((3, 16)),
            dma((2, 3)), dma((2, 3)), dma((2,)), dma((2,)), dma((3,)), dma((8,)), dma((3,)),
        ],
        compiler_params=pltpu.CompilerParams(
            collective_id=0, has_side_effects=True, vmem_limit_bytes=56 << 20),
        name="rotate_and_filter",
    )(orbitals, rotation, potential, weights)
    return out.reshape(24, 8, NXY)


def solution(mesh):
    in_specs = (P("band", None, "dom"), P("band", None), P("dom", None), P())
    out_specs = P("band", "dom", None)
    run = jax.shard_map(body, mesh=mesh, in_specs=in_specs, out_specs=out_specs, check_vma=False)

    def whole(orbitals, rotation, potential):
        return run(orbitals, rotation, potential, jnp.asarray(y_weights(), BF16))

    return whole
```

```python
import jax
import jax.numpy as jnp
import numpy as np
from jax import lax
from jax.experimental import pallas as pl
from jax.experimental.pallas import tpu as pltpu
from jax.sharding import PartitionSpec as P

NXY = 3200
MESH = pl.DeviceIdType.MESH
F32 = jnp.float32
BF16 = jnp.bfloat16
LANES = 128

potential_offset = 0.5
near_weight = 2.0 / 3.0
half_range = 4.25


def target_domain(h, y, z, c, half):
    return lax.rem(h + half, 2) * 8 + lax.rem(z + y + c + 2 * half, 4) * 2 + half


def kernel(
    orb_hbm, rot_hbm, pot_hbm, wy_ref,
    out_hbm,
    orb, rot, pot, wide, planes, send1, recv1, send2, weights,
    own, low, high, pown, plow, phigh,
    even, odd, ring0, ring1, scaled, done,
    s1, r1, s2, r2, sh, rh, sp, rp, ls, li, lo,
):
    band, dom = lax.axis_index("band"), lax.axis_index("dom")
    h, y = band // 4, lax.rem(band, 4)
    x, z, c = dom // 8, lax.rem(dom // 2, 4), lax.rem(dom, 2)
    mirror = (1 - x) * 8 + z * 2 + c
    has_low, has_high = dom > 0, dom < 15
    up, down = lax.rem(dom + 1, 16), lax.rem(dom + 15, 16)

    def partner(k):
        return lax.rem(h + k // 4, 2) * 4 + lax.rem(y + lax.rem(k, 4), 4)

    def load(i):
        return pltpu.make_async_copy(orb_hbm.at[pl.ds(4 * i, 4)], orb.at[pl.ds(4 * i, 4)], li.at[i])

    load_rot = pltpu.make_async_copy(rot_hbm, rot, li.at[6])
    load_pot = pltpu.make_async_copy(pot_hbm, pot, li.at[7])
    for i in range(6):
        load(i).start()
    load_rot.start()
    load_pot.start()

    barrier = pltpu.get_barrier_semaphore()

    def greet(b, d):
        pl.semaphore_signal(barrier, inc=1, device_id={"band": b, "dom": d}, device_id_type=MESH)

    greet(band, up)
    greet(band, down)
    for k in range(8):
        greet(partner(k), mirror)
    for q in range(16):
        qz, qc = (q // 2) % 4, q % 2
        greet(lax.rem(x + c, 2) * 4 + lax.rem(z - qz - qc - 2 * c + 16, 4), q)
    turn = (dom // 2) * 16
    lane = lax.broadcasted_iota(jnp.int32, (8, LANES), 1)
    block = lane // 16
    lane24 = lax.broadcasted_iota(jnp.int32, (24, LANES), 1)
    block24 = lane24 // 16

    for i in range(6):
        load(i).wait()

        def widen(o, _):
            rows = pl.ds(pl.multiple_of(o * 128, 128), 128)
            v = orb[o].astype(F32)
            v = jnp.where(c == 0, v, jnp.concatenate([v[8:], v[:8]], axis=0))
            for j, w in enumerate((v[:LANES], jnp.concatenate([v[LANES:], v[: 256 - 200]], axis=0))):
                wide[j, rows, :] = jnp.transpose(w)
            return 0

        lax.fori_loop(4 * i, 4 * i + 4, widen, 0)

    def by_plane(d, _):
        for zz in range(8):
            first = pl.multiple_of(192 * d + 24 * zz, 8)
            for j in range(2):
                v = wide[j, pl.ds(8 * d + zz, 24, stride=128), :]
                planes[j, pl.ds(first, 24), :] = pltpu.roll(v, lax.rem(turn + 16 * zz, 128), 1)
        return 0

    lax.fori_loop(0, 16, by_plane, 0)
    load_rot.wait()
    r = rot[...].astype(F32)
    r_left = r[:, :LANES]
    r_right = jnp.concatenate([r[:, LANES:], r[:, : 256 - 192]], axis=1)

    def pack(u, half, k):
        to = partner(k)
        first = target_domain(to // 4, lax.rem(to, 4), z, c, half) * 192
        v = None
        for zz in range(8):
            s = planes[u // 8, pl.ds(pl.multiple_of(first + 24 * zz, 8), 24), :]
            v = s if v is None else jnp.where(block24 == lax.rem(u + zz + dom // 2, 8), s, v)
        return v

    def put(k, t, a, b):
        send1[k, t, 0] = a[:16].astype(BF16)
        send1[k, t, 1] = b[:16].astype(BF16)
        send1[k, t, 2] = jnp.concatenate([a[16:], b[16:]], axis=0).astype(BF16)

    def copy1(slot, source, part, to):
        rows = pl.ds(2 * part, 2)
        return pltpu.make_async_remote_copy(
            src_ref=send1.at[slot, rows], dst_ref=recv1.at[source, rows],
            send_sem=s1.at[part, slot], recv_sem=r1.at[part, source],
            device_id={"band": to, "dom": mirror}, device_id_type=MESH)

    pl.semaphore_wait(barrier, 26)

    def ends(k, _):
        put(k, 0, *[pltpu.roll(pack(12, half, k), 8 * c, 1) for half in range(2)])
        put(k, 1, r_left, r_right)
        copy1(k, band, 0, partner(k)).start()
        return 0

    lax.fori_loop(0, 8, ends, 0)

    def units(i, _):
        part, k = i // 8 + 1, lax.rem(i, 8)
        for j in range(2):
            u = 2 * part - 2 + j
            put(k, u + 2, *[pack(u, half, k) for half in range(2)])
        copy1(k, band, part, partner(k)).start()
        return 0

    lax.fori_loop(0, 48, units, 0)

    load_pot.wait()
    for t in range(25):
        v = None
        for p in range(8):
            tile = (25 * p + t) // 8
            s = pot[:, 128 * tile : 128 * tile + 128]
            v = s if v is None else jnp.where(block == (p + t) % 8, s, v)
        if t % 8:
            v = pltpu.roll(v, 128 - 16 * (t % 8), 1)
        pown[t] = (v - potential_offset) * (2.0 / half_range)

    pot_copies = []
    for i, (dst, to, ok) in enumerate(((plow, up, has_high), (phigh, down, has_low))):
        cp = pltpu.make_async_remote_copy(
            src_ref=pown, dst_ref=dst, send_sem=sp.at[i], recv_sem=rp.at[i],
            device_id={"band": band, "dom": to}, device_id_type=MESH)
        pot_copies.append(cp)
        pl.when(ok)(cp.start)

    for k in range(8):
        copy1(k, k, 0, band).wait_recv()
    zero = jnp.zeros((8, 2 * LANES), F32)
    first_rows = jnp.concatenate([
        recv1[:, 1, 0].astype(F32).reshape(128, LANES),
        recv1[:, 1, 1].astype(F32).reshape(128, LANES)], axis=1)
    for half in range(2):
        rows = [first_rows]
        for k in range(8):
            m = recv1[k, 1, 2].astype(F32)
            m = jnp.concatenate([m[:8], m[8:]], axis=1)
            rows += [m, zero] if half == 0 else [zero, m]
        weights[half] = jnp.transpose(jnp.concatenate(rows, axis=0))[:192].astype(BF16)

    def rhs(t, half):
        return jnp.concatenate(
            [recv1[:, t, half].reshape(128, LANES), recv1[:, t, 2].reshape(128, LANES)], axis=0)

    is_odd_half = lax.rem(lane // 8, 2)
    for half in range(2):
        out = jnp.dot(weights[half], rhs(0, half), preferred_element_type=F32)
        for b in range(8):
            v = out[24 * b : 24 * b + 24]
            first = jnp.where(is_odd_half == c, v[:8], pltpu.roll(v[16:], jnp.where(c == 0, 8, 120), 1))
            send2[half * 8 + b, 0, 6] = jnp.concatenate([first, v[8:16]], axis=0).astype(BF16)

    def rotate(part, _):
        for k in range(8):
            copy1(k, k, part, band).wait_recv()
        for half in range(2):
            both = jnp.concatenate([rhs(2 * part, half), rhs(2 * part + 1, half)], axis=1)
            out = jnp.dot(weights[half], both, preferred_element_type=F32)
            for b in range(8):
                for g in range(3):
                    v = out[24 * b + 8 * g : 24 * b + 8 * g + 8]
                    v = jnp.concatenate([v[:, :LANES], v[:, LANES:]], axis=0)
                    send2[half * 8 + b, g, part - 1] = v.astype(BF16)
        return 0

    lax.fori_loop(1, 7, rotate, 0)

    def tiles(g):
        return pl.ds(0, 7 if g == 0 else 6)

    def copy2(slot, source, g, b, d):
        return pltpu.make_async_remote_copy(
            src_ref=send2.at[slot, g, tiles(g)], dst_ref=own.at[g, source, tiles(g)],
            send_sem=s2.at[g, slot], recv_sem=r2.at[g, source],
            device_id={"band": b, "dom": d}, device_id_type=MESH)

    def keep(slot, source, g):
        return pltpu.make_async_copy(send2.at[slot, g, tiles(g)], own.at[g, source, tiles(g)], ls.at[g])

    def is_self(half):
        return target_domain(h, y, z, c, half) == dom

    for g in range(3):
        def post(i, _):
            half, k = i // 8, lax.rem(i, 8)
            to, to_dom = partner(k), target_domain(h, y, z, c, half)
            here = jnp.logical_and(to_dom == dom, k == 0)

            @pl.when(jnp.logical_not(here))
            def _():
                copy2(half * 8 + to, mirror, g, to, to_dom).start()

            @pl.when(here)
            def _():
                keep(half * 8 + to, mirror, g).start()

            return 0

        lax.fori_loop(0, 16, post, 0)

    self_sent = jnp.logical_or(is_self(0), is_self(1))

    def halo(i, g):
        dst, to = ((low, up), (high, down))[i]
        return pltpu.make_async_remote_copy(
            src_ref=own.at[g, :, tiles(g)], dst_ref=dst.at[g, :, tiles(g)], send_sem=sh.at[i, g], recv_sem=rh.at[i, g],
            device_id={"band": band, "dom": to}, device_id_type=MESH)

    def arrive(g):
        def one(q, _):
            here = jnp.logical_and(self_sent, mirror == q)

            @pl.when(jnp.logical_not(here))
            def _():
                copy2(q, q, g, band, dom).wait_recv()

            @pl.when(here)
            def _():
                keep(0, q, g).wait()

            return 0

        lax.fori_loop(0, 16, one, 0)
        pl.when(has_high)(halo(0, g).start)
        pl.when(has_low)(halo(1, g).start)

    inside = (has_low, None, has_high)
    for i, ok_send, ok_recv in ((0, has_high, has_low), (1, has_low, has_high)):
        pl.when(ok_recv)(pot_copies[i].wait_recv)

    for region, ref in enumerate((plow, pown, phigh)):
        def spread(t, _):
            v = ref[t]
            if inside[region] is not None:
                v = jnp.where(inside[region], v, 0.0)
            for zz in range(8):
                rows = slice(64 * region + 8 * zz, 64 * region + 8 * zz + 8)
                scaled[t, rows, :] = jnp.broadcast_to(v[zz : zz + 1], (8, LANES))
            return 0

        lax.fori_loop(0, 25, spread, 0)

    b_all = -near_weight * 2.0 / half_range
    b_low = jnp.where(has_low, b_all, 0.0)
    b_high = jnp.where(has_high, b_all, 0.0)
    rings = (ring0, ring1)

    def to_ring(ring, t, rows, v):
        xl, yh = t // 5, t % 5
        for pos in {0: (1, 6), 1: (2, 7), 4: (5, 0)}.get(yh, (yh + 1,)):
            ring[xl, rows, 128 * pos : 128 * pos + 128] = v

    def unpack(region, ref, g):
        def finish(t, zz, pair):
            if inside[region] is not None:
                pair = [jnp.where(inside[region], v, 0.0) for v in pair]
            v = jnp.concatenate(pair, axis=0)
            rows = slice(64 * region + 8 * zz, 64 * region + 8 * zz + 16)
            even[t, rows, :] = v
            to_ring(ring0, t, rows, v.astype(BF16))

        for e in range(2):
            for i in range(6):
                src = [ref[g, 2 * p + e, i].astype(F32) for p in range(8)]
                for j in range(2):
                    u = 2 * i + j
                    for zz in range(0, 8, 2):
                        pair = []
                        for s in (u + zz, u + zz + 1):
                            v = src[0][8 * j : 8 * j + 8]
                            for p in range(1, 8):
                                v = jnp.where(block == (s + p) % 8, src[p][8 * j : 8 * j + 8], v)
                            pair.append(pltpu.roll(v, 128 - 16 * (s % 8), 1) if s % 8 else v)
                        finish(13 * e + u, zz, pair)
        src = []
        for d in range(16):
            v = ref[0, d, 6].astype(F32)
            v = jnp.where(g == 1, v[8:], v[:8])
            src.append(jnp.where(g == 2, pltpu.roll(v, 8 if d % 2 else 120, 1), v))
        for zz in range(0, 8, 2):
            pair = []
            for s in (12 + zz, 13 + zz):
                v = src[0]
                for d in range(1, 16):
                    v = jnp.where(lane // 8 == 2 * ((s + d // 2) % 8) + d % 2, src[d], v)
                pair.append(pltpu.roll(v, 128 - 16 * (s % 8), 1) if s % 8 else v)
            finish(12, zz, pair)

    def step(order, g):
        a, b = 2 * order + 2, 22 - 2 * order
        now, other = (even, odd) if order % 2 == 0 else (odd, even)
        ring, following = rings[order % 2], rings[(order + 1) % 2]
        count = 8 * (b - a)
        for n in range(3):
            window = jnp.concatenate(
                [ring[xl, 8 * a : 8 * b, 256 * n : 256 * n + 512] for xl in range(5)], axis=0)
            width = 256 if n < 2 else 128
            planar = jnp.dot(window, wy_ref[:, :width], preferred_element_type=F32)
            for l in range(width // 128):
                yh = 2 * n + l
                v = {q: [now[5 * xl + yh, 8 * q : 8 * q + 8, :] for xl in range(5)] for q in range(a - 2, b + 2)}
                pending = None
                for q in range(a, b):
                    m = v[q]
                    before = [pltpu.roll(m[3], 16, 1), pltpu.roll(m[4], 16, 1)]
                    after = [pltpu.roll(m[0], 112, 1), pltpu.roll(m[1], 112, 1)]
                    line = before + m + after
                    coef = b_low if q < 8 else (b_all if q < 16 else b_high)
                    news = []
                    for xl in range(5):
                        t = 5 * xl + yh
                        near = (line[xl + 1] + line[xl + 3]) + (v[q - 1][xl] + v[q + 1][xl])
                        far = (line[xl] + line[xl + 4]) + (v[q - 2][xl] + v[q + 2][xl])
                        rows = slice(8 * q, 8 * q + 8)
                        first = count * xl + 8 * (q - a)
                        total = planar[first : first + 8, 128 * l : 128 * l + 128] + near - far * (1.0 / 16.0)
                        new = scaled[t, rows, :] * m[xl] + coef * total
                        if order == 0:
                            new = new * 0.5
                        else:
                            new = new - other[t, rows, :]
                        if order < 3:
                            other[t, rows, :] = new
                        else:
                            done[g, 64 * t + 8 * (q - 8) : 64 * t + 8 * (q - 8) + 8, :] = new
                        news.append(new)
                    if order < 3:
                        if q % 2:
                            for xl in range(5):
                                to_ring(following, 5 * xl + yh, slice(8 * q - 8, 8 * q + 8),
                                        jnp.concatenate([pending[xl], news[xl]], axis=0).astype(BF16))
                        pending = news

    def write(g):
        return pltpu.make_async_copy(done.at[g], out_hbm.at[g], lo.at[g])

    arrive(0)

    def group(g, _):
        for nxt in (1, 2):
            @pl.when(g == nxt - 1)
            def _():
                arrive(nxt)

        for now in range(3):
            @pl.when(g == now)
            def _():
                pl.when(has_low)(halo(0, now).wait_recv)
                pl.when(has_high)(halo(1, now).wait_recv)

        for region, ref in enumerate((low, own, high)):
            unpack(region, ref, g)
        for order in range(4):
            step(order, g)
        write(g).start()
        return 0

    lax.fori_loop(0, 3, group, 0)

    def drain1(i, _):
        copy1(lax.rem(i, 8), 0, i // 8, band).wait_send()
        return 0

    lax.fori_loop(0, 56, drain1, 0)
    for g in range(3):
        def drain2(slot, _):
            here = jnp.logical_and(target_domain(h, y, z, c, slot // 8) == dom, lax.rem(slot, 8) == band)

            @pl.when(jnp.logical_not(here))
            def _():
                copy2(slot, 0, g, band, dom).wait_send()

            return 0

        lax.fori_loop(0, 16, drain2, 0)
        pl.when(has_high)(halo(0, g).wait_send)
        pl.when(has_low)(halo(1, g).wait_send)
    pl.when(has_high)(pot_copies[0].wait_send)
    pl.when(has_low)(pot_copies[1].wait_send)
    for g in range(3):
        write(g).wait()


def order_kernel(done, out_ref):
    block = lax.broadcasted_iota(jnp.int32, (8, LANES), 1) // 16

    def orbital(o, _):
        v = []
        for t in range(25):
            s = done[0, pl.ds(64 * t + o, 8, stride=8), :]
            v.append(pltpu.roll(s, 16 * (t % 8), 1) if t % 8 else s)
        rows = pl.ds(pl.multiple_of(8 * o, 8), 8)
        for tau in range(25):
            s = v[8 * tau % 25]
            for beta in range(1, 8):
                s = jnp.where(block == beta, v[(8 * tau + beta) % 25], s)
            out_ref[rows, 128 * tau : 128 * tau + 128] = s
        return 0

    lax.fori_loop(0, 8, orbital, 0)


def y_weights():
    out = np.zeros((512, 256), np.float32)
    for col in range(256):
        j, p, yl = col // 128, col % 128 // 16, col % 16
        for step, value in ((1, 1.0), (2, -1.0 / 16.0)):
            for sign in (-1, 1):
                at = yl + sign * step
                out[128 * (1 + j + at // 16) + 16 * p + at % 16, col] += value
    return out


def body(orbitals, rotation, potential, weights):
    anyspace = pl.BlockSpec(memory_space=pl.ANY)
    dma = pltpu.SemaphoreType.DMA
    group = pltpu.VMEM((3, 16, 7, 16, LANES), BF16)
    plane = pltpu.VMEM((25, 8, LANES), F32)
    field = pltpu.VMEM((25, 192, LANES), F32)
    ring = pltpu.VMEM((5, 192, 1024), BF16)
    parts = pltpu.VMEM((8, 14, 3, 16, LANES), BF16)
    done = pl.pallas_call(
        kernel,
        out_shape=jax.ShapeDtypeStruct((3, 25 * 64, LANES), F32),
        in_specs=[anyspace, anyspace, anyspace, pl.BlockSpec(memory_space=pltpu.VMEM)],
        out_specs=anyspace,
        scratch_shapes=[
            pltpu.VMEM((24, 200, 128), BF16),
            pltpu.VMEM((24, 192), BF16),
            pltpu.VMEM((8, NXY), F32),
            pltpu.VMEM((2, 24 * 128, LANES), F32),
            pltpu.VMEM((2, 128 * 24, LANES), F32),
            parts, parts,
            pltpu.VMEM((16, 3, 7, 16, LANES), BF16),
            pltpu.VMEM((2, 192, 256), BF16),
            group, group, group,
            plane, plane, plane,
            field, field, ring, ring, field,
            pltpu.VMEM((3, 25 * 64, LANES), F32),
            dma((7, 8)), dma((7, 8)), dma((3, 16)), dma((3, 16)),
            dma((2, 3)), dma((2, 3)), dma((2,)), dma((2,)), dma((3,)), dma((8,)), dma((3,)),
        ],
        compiler_params=pltpu.CompilerParams(
            collective_id=0, has_side_effects=True, vmem_limit_bytes=56 << 20),
        name="rotate_and_filter",
    )(jnp.swapaxes(orbitals, 1, 2), rotation, potential, weights)
    out = pl.pallas_call(
        order_kernel,
        grid=(3,),
        out_shape=jax.ShapeDtypeStruct((192, NXY), F32),
        in_specs=[pl.BlockSpec((1, 25 * 64, LANES), lambda g: (g, 0, 0))],
        out_specs=pl.BlockSpec((64, NXY), lambda g: (g, 0)),
        name="order",
    )(done)
    return out.reshape(24, 8, NXY)


def solution(mesh):
    in_specs = (P("band", None, "dom"), P("band", None), P("dom", None), P())
    out_specs = P("band", "dom", None)
    run = jax.shard_map(body, mesh=mesh, in_specs=in_specs, out_specs=out_specs, check_vma=False)

    def whole(orbitals, rotation, potential):
        return run(orbitals, rotation, potential, jnp.asarray(y_weights(), BF16))

    return whole
```
